128 devices in a mesh: chan: 64 (over x_lo, y, z, core), tm: 2 (over x_hi).
Axes of the slice: x: 4 (x_hi: 2, x_lo: 2; x = x_hi * 2 + x_lo), y: 4, z: 4, core: 2. Of those that a mesh axis runs over, the one named last changes fastest.
Arguments:
- voltages: bfloat16 [2048, 131840], P('chan', 'tm'), may hold values from -6 to 6
- kept: int32 [64], replicated, may hold values from 0 to 64, as said below
- assign: int32 [2048], replicated, may hold values from 0 to 2047, each once
Outputs:
- visibility: bfloat16 [64, 2048, 2, 2048], P('chan', 'tm')
The draws below stay inside these ranges and needn't reach their ends.
Inputs may be any that keep to these rules, and one draw needn't show every extreme that they name: `kept`: distinct bins.
All inputs are finite; a program needn't handle non-finite values.
Results may differ from the reference program's by a relative error of at most 0.0062.
Values may be sent and summed in bfloat16 or wider, within the bound.
A program may use at most 192 MiB of HBM per device.

```python
import jax
import jax.numpy as jnp
from jax import lax

NFFT = 128
TAPS = 4
SPEC_DEV = 512
SAMP_DEV = 65920
INPUTS = 2048
CHANNELS = 64
TOTAL_SPEC = 1024


def draw_kept(key, part):
    order = jax.random.permutation(key, NFFT // 2 + 1)
    return order[:CHANNELS].astype(jnp.int32)


def levels(stream_key, shape, shards, least, high):
    factor_of = 1.0
    for axis_at, blocks in shards:
        heights = jax.random.uniform(jax.random.fold_in(jax.random.fold_in(stream_key, 6), axis_at), (blocks,), jnp.float32, least / len(shards), high / len(shards))
        factor_of = factor_of * jnp.repeat(jnp.exp(heights), shape[axis_at] // blocks).reshape((-1,) + (1,) * (len(shape) - 1 - axis_at))
    return factor_of


def normal_values(own_key, extent, spread, most, cuts=(), held_as=jnp.bfloat16):
    array = spread * jax.random.normal(own_key, extent, jnp.float32)
    if cuts:
        array = array * levels(own_key, extent, cuts, -0.22, 0.18)
    return jnp.clip(array, -most, most).astype(held_as)


def setup_inputs(seed: int = 0) -> dict:
    seeds = jax.random.split(jax.random.key(seed), 4)
    voltages = normal_values(seeds[0], (INPUTS, TOTAL_SPEC // SPEC_DEV * SAMP_DEV), 1.0, 6.0, ((0, 64), (1, 2)))
    kept = draw_kept(jax.random.fold_in(seeds[3], 71), 0)
    assign = jax.random.permutation(seeds[2], INPUTS).astype(jnp.int32)
    return {"voltages": voltages, "kept": kept, "assign": assign}


def filter_coeffs(kept, tap_count, points):
    length = tap_count * points
    places = jnp.arange(length, dtype=jnp.int32)
    positions = places.astype(jnp.float32)
    window = jnp.sinc((positions - (length - 1) / 2.0) / points) * (0.54 - 0.46 * jnp.cos(2.0 * jnp.pi * positions / (length - 1)))
    factor = 1.0 / jnp.sqrt(jnp.sum(window * window))
    phase_index = places[:, None] % points * kept[None, :] % points
    angles = 2.0 * jnp.pi * phase_index.astype(jnp.float32) / points
    paired = jnp.stack([jnp.cos(angles), -jnp.sin(angles)], axis=2) * (window * factor)[:, None, None]
    return paired.reshape(length, 2 * kept.shape[0]).astype(jnp.bfloat16)

def reference(voltages, kept, assign):
    coeffs = filter_coeffs(kept, TAPS, NFFT).astype(jnp.float32)
    block_count = TOTAL_SPEC // SPEC_DEV
    blocks = voltages.reshape(INPUTS, block_count, SPEC_DEV + TAPS - 1, NFFT)
    blocks = jnp.moveaxis(blocks, 1, 0)

    def channelize(time_block):
        frames = time_block.astype(jnp.float32)
        summed = jnp.zeros((2 * CHANNELS, INPUTS, SPEC_DEV), jnp.float32)
        for tap_index in range(TAPS):
            summed = summed + jnp.einsum('isn,nc->cis', frames[:, tap_index:tap_index + SPEC_DEV], coeffs[tap_index * NFFT:(tap_index + 1) * NFFT], precision=lax.Precision.HIGHEST)
        return summed.astype(jnp.bfloat16)
    spectra = lax.map(channelize, blocks)
    spectra = spectra.reshape(block_count, CHANNELS, 2, INPUTS, SPEC_DEV)
    spectra = jnp.transpose(spectra, (1, 2, 3, 0, 4)).reshape(CHANNELS, 2, INPUTS, TOTAL_SPEC)
    slot_of = jnp.zeros((INPUTS,), jnp.int32).at[assign].set(jnp.arange(INPUTS, dtype=jnp.int32))

    def correlate(channel):
        ordered = jnp.take(channel, slot_of, axis=1).astype(jnp.float32)
        lefthand = jnp.concatenate([ordered[0], ordered[1]], axis=1)
        flipped = jnp.concatenate([-ordered[1], ordered[0]], axis=1)
        righthand = jnp.concatenate([lefthand, flipped], axis=0)
        visible = jnp.dot(lefthand, righthand.T, precision=lax.Precision.HIGHEST, preferred_element_type=jnp.float32) * (1.0 / TOTAL_SPEC)
        return visible.reshape(INPUTS, 2, INPUTS).astype(jnp.bfloat16)
    return lax.map(correlate, spectra)
```

```python
import jax
import jax.numpy as jnp
import numpy as np
from jax import lax
from jax.experimental import pallas as pl
from jax.experimental.pallas import tpu as pltpu
from jax.sharding import PartitionSpec as P

NFFT = 128
TAPS = 4
SPEC_DEV = 512
SAMP_DEV = 65920
INPUTS = 2048
CHANNELS = 64
ROWS = 1024
LOCAL = 32
PARTS = 4
CHUNK = SPEC_DEV // PARTS
WIDE = 2 * CHUNK
MESH = pl.DeviceIdType.MESH
BF = jnp.bfloat16
F32 = jnp.float32


def coefficients(kept):
    length = TAPS * NFFT
    at = np.arange(length, dtype=np.float64)
    window = np.sinc((at - (length - 1) / 2.0) / NFFT) * (
        0.54 - 0.46 * np.cos(2.0 * np.pi * at / (length - 1))
    )
    window = jnp.asarray(window / np.sqrt(np.sum(window * window)), F32)
    places = jnp.arange(length, dtype=jnp.int32) % NFFT
    quarter = jnp.array([0, NFFT // 4], jnp.int32)
    turns = (places[None, None, :] * kept[None, :, None] + quarter[:, None, None]) % NFFT
    angles = turns.astype(F32) * (2.0 * np.pi / NFFT)
    return (jnp.cos(angles) * window).astype(BF).reshape(2 * CHANNELS, length)


def contract_lanes(left, right):
    return lax.dot_general(left, right, (((1,), (1,)), ((), ())), preferred_element_type=F32)


def dot(left, right):
    return jnp.dot(left, right, preferred_element_type=F32)


def main_kernel(
    volt_hbm,
    coef,
    assign,
    out_hbm,
    volt,
    perm,
    frames,
    chan,
    sendbuf,
    near,
    slab_a,
    slab_b,
    slab_c,
    onehot,
    right,
    left,
    acc,
    stage,
    volt_sem,
    near_send,
    near_recv,
    slab_send,
    slab_recv,
    out_sem,
):
    me = lax.axis_index("chan")
    half = lax.axis_index("tm")
    low = me // 32
    y = (me // 8) % 4
    z = (me // 2) % 4
    core = me % 2
    place = me % 32

    def volt_copy(q):
        first = 0 if q == 0 else (q * CHUNK + 3) * NFFT
        last = ((q + 1) * CHUNK + 3) * NFFT
        part = pl.ds(first, last - first)
        return pltpu.make_async_copy(volt_hbm.at[:, part], volt.at[:, part], volt_sem.at[q])

    for q in range(PARTS):
        volt_copy(q).start()

    def near_device(dy, dz, dc):
        there = (((y + dy) % 4) * 4 + (z + dz) % 4) * 2 + (core + dc) % 2
        return there

    barrier = pltpu.get_barrier_semaphore()

    def greet(k, carry):
        there = near_device(k // 8, (k // 2) % 4, k % 2)
        pl.semaphore_signal(
            barrier, inc=1, device_id=(low * 32 + there, half), device_id_type=MESH
        )
        return carry

    lax.fori_loop(1, 32, greet, 0)
    far = (
        ((1 - low) * 32 + place, half),
        ((1 - low) * 32 + place, 1 - half),
        (low * 32 + place, 1 - half),
    )
    for device in far:
        pl.semaphore_signal(barrier, inc=1, device_id=device, device_id_type=MESH)

    row = lax.broadcasted_iota(jnp.int32, (256, 256), 0)
    col = lax.broadcasted_iota(jnp.int32, (256, 256), 1)
    perm[...] = jnp.where(col == (row & 15) * 16 + (row >> 4), 1.0, 0.0).astype(BF)

    def channelize(q):
        volt_copy(q).wait()
        for ih in range(2):

            def reorder(sb, carry):
                base = (q * CHUNK + sb * 16) * NFFT
                pieces = [
                    volt[ih * 16 : ih * 16 + 16, pl.ds(pl.multiple_of(base + s * NFFT, NFFT), 4 * NFFT)]
                    for s in range(16)
                ]
                moved = dot(perm[...], jnp.concatenate(pieces, axis=0)).astype(BF)
                frames[:, pl.ds(pl.multiple_of(sb * 16, 16), 16), :] = moved.reshape(16, 16, 4 * NFFT)
                return carry

            lax.fori_loop(0, CHUNK // 16, reorder, 0)

            def transform(ip, carry):
                pair = frames[pl.ds(ip * 2, 2)].reshape(2 * CHUNK, 4 * NFFT)
                found = contract_lanes(coef[...], pair).astype(BF)
                for i in range(2):
                    for p in range(2):
                        chan[ip * 2 + i, :, p * CHUNK : (p + 1) * CHUNK] = found[
                            p * CHANNELS : (p + 1) * CHANNELS, i * CHUNK : (i + 1) * CHUNK
                        ]
                return carry

            lax.fori_loop(0, 8, transform, 0)

            for cb in range(4):
                block = chan[:, cb * 16 : cb * 16 + 16, :].reshape(256, WIDE)
                moved = dot(perm[...], block).astype(BF).reshape(16, 16, WIDE)
                sendbuf[q, cb // 2, (cb % 2) * 16 : (cb % 2) * 16 + 16, ih * 16 : ih * 16 + 16, :] = moved

    my_rows = pl.ds(pl.multiple_of(place * LOCAL, LOCAL), LOCAL)

    def self_copy(q):
        return pltpu.make_async_copy(
            sendbuf.at[q, :, place], near.at[q, :, my_rows], near_recv.at[q, y]
        )

    def near_copy(q, dy, dz, dc):
        there = near_device(dy, dz, dc)
        return pltpu.make_async_remote_copy(
            src_ref=sendbuf.at[q, :, there],
            dst_ref=near.at[q, :, my_rows],
            send_sem=near_send.at[q],
            recv_sem=near_recv.at[q, y],
            device_id=(low * 32 + there, half),
            device_id_type=MESH,
        )

    def send_near(q):
        self_copy(q).start()
        if q == 0:

            def first(k, carry):
                near_copy(q, 0, k // 2, k % 2).start()
                return carry

            lax.fori_loop(1, 8, first, 0)

            def second(k, carry):
                near_copy(q, 1 + 2 * (k % 2), (k // 2) % 4, k // 8).start()
                return carry

            lax.fori_loop(0, 16, second, 0)

            def third(k, carry):
                near_copy(q, 2, k // 2, k % 2).start()
                return carry

            lax.fori_loop(0, 8, third, 0)
        else:

            def some(k, carry):
                o = (k * 11) % 32
                near_copy(q, o % 4, (o // 4) % 4, o // 16).start()
                return carry

            lax.fori_loop(1, 32, some, 0)

    def slab_copy(q, group, kind):
        rows = pl.ds(pl.multiple_of(group * 256, 256), 256)
        which = low if kind == 2 else 1 - low
        slab = (slab_a, slab_b, slab_c)[kind]
        return pltpu.make_async_remote_copy(
            src_ref=near.at[q, which, rows],
            dst_ref=slab.at[q, rows],
            send_sem=slab_send.at[q],
            recv_sem=slab_recv.at[q, kind],
            device_id=far[kind],
            device_id_type=MESH,
        )

    def wait_group(q, group):
        rows = pl.ds(pl.multiple_of(group * 256, 256), 256)
        block = near.at[q, :, rows]
        pltpu.make_async_copy(block, block, near_recv.at[q, group]).wait()

    def forward_group(q, step):
        group = (y + (0, 1, 3, 2)[step]) % 4
        wait_group(q, group)
        for kind in range(3):
            slab_copy(q, group, kind).start()

    def forward(q):
        for step in range(4):
            wait_group(q, (y + step) % 4)
        for step in range(4):
            for kind in range(2):
                slab_copy(q, step, kind).start()
        for step in range(4):
            slab_copy(q, step, 2).start()

    def wait_slab(q, kind):
        block = (slab_a, slab_b, slab_c)[kind].at[q]
        pltpu.make_async_copy(block, block, slab_recv.at[q, kind]).wait()

    def reorder_inputs(mine, other):
        def part(t, carry):
            rows = pl.ds(pl.multiple_of(t * 512, 512), 512)
            total = dot(onehot[low, rows, :], mine[...]) + dot(onehot[1 - low, rows, :], other[...])
            right[rows, :] = total.astype(BF)
            return carry

        lax.fori_loop(0, INPUTS // 512, part, 0)

        def take(t, carry):
            rows = pl.ds(pl.multiple_of(half * ROWS + t * 256, 256), 256)
            block = right[rows, :]
            upper = pl.ds(pl.multiple_of(t * 256, 256), 256)
            lower = pl.ds(pl.multiple_of(ROWS + t * 256, 256), 256)
            left[upper, :] = block
            left[lower, :CHUNK] = block[:, CHUNK:]
            left[lower, CHUNK:] = -block[:, :CHUNK]
            return carry

        lax.fori_loop(0, ROWS // 256, take, 0)

    def correlate():
        def tile(n, carry):
            columns = right[pl.ds(pl.multiple_of(n * 256, 256), 256), :]
            for m in range(4):
                rows = slice(m * 512, (m + 1) * 512)
                acc[n, rows, :] += contract_lanes(left[rows, :], columns)
            return carry

        lax.fori_loop(0, 8, tile, 0)

    def out_copy(n, slot):
        columns = pl.ds(pl.multiple_of(n * 256, 256), 256)
        return pltpu.make_async_copy(stage.at[slot], out_hbm.at[:, columns], out_sem.at[slot])

    def finish():
        def tile(n, carry):
            slot = n % 2

            @pl.when(n >= 2)
            def _():
                out_copy(n - 2, slot).wait()

            columns = right[pl.ds(pl.multiple_of(n * 256, 256), 256), :]
            for m in range(4):
                rows = slice(m * 512, (m + 1) * 512)
                total = acc[n, rows, :] + contract_lanes(left[rows, :], columns)
                stage[slot, rows, :] = (total * (1.0 / 1024.0)).astype(BF)
            out_copy(n, slot).start()
            return carry

        lax.fori_loop(0, 8, tile, 0)
        out_copy(6, 0).wait()
        out_copy(7, 1).wait()

    def own_half(q):
        wait_slab(q, 0)
        reorder_inputs(near.at[q, low], slab_a.at[q])

    def other_half(q):
        wait_slab(q, 1)
        wait_slab(q, 2)
        reorder_inputs(slab_c.at[q], slab_b.at[q])

    channelize(0)
    pl.semaphore_wait(barrier, 34)
    send_near(0)
    forward_group(0, 0)
    channelize(1)
    send_near(1)
    for step in range(1, 4):
        forward_group(0, step)
    channelize(2)
    send_near(2)
    channelize(3)
    send_near(3)

    def fill(t, carry):
        rows = pl.ds(pl.multiple_of(t * 256, 256), 256)
        antenna = t * 256 + lax.broadcasted_iota(jnp.int32, (256, ROWS), 0)
        for s in range(2):
            same = antenna == assign[:, s * ROWS : (s + 1) * ROWS]
            onehot[s, rows, :] = jnp.where(same, 1.0, 0.0).astype(BF)
        acc[t] = jnp.zeros((INPUTS, 256), F32)
        return carry

    lax.fori_loop(0, 8, fill, 0)
    forward(1)
    own_half(0)
    correlate()
    other_half(0)
    correlate()
    forward(2)
    forward(3)

    def middle(q, carry):
        own_half(q)
        correlate()
        other_half(q)
        correlate()
        return carry

    lax.fori_loop(1, 3, middle, 0)
    own_half(3)
    correlate()
    other_half(3)
    finish()

    for q in range(PARTS):
        sent = sendbuf.at[q, :, pl.ds(0, 31)]
        pltpu.make_async_copy(sent, sent, near_send.at[q]).wait()
        for slab in (slab_a, slab_b, slab_c):
            pltpu.make_async_copy(slab.at[q], slab.at[q], slab_send.at[q]).wait()


def place_kernel(perm, x, o):
    def body(g, carry):
        rows = pl.ds(pl.multiple_of(g * 16, 16), 16)
        for jh in range(2):
            parts = [
                x[p, rows, (jh * 8 + j) * 128 : (jh * 8 + j + 1) * 128]
                for j in range(8)
                for p in range(2)
            ]
            moved = dot(perm[...], jnp.concatenate(parts, axis=0)).astype(BF)
            o[rows, jh * 16 : (jh + 1) * 16, :] = moved.reshape(16, 16, 128)
        return carry

    lax.fori_loop(0, x.shape[1] // 16, body, 0)


def shards(voltages, kept, assign):
    coef = coefficients(kept)
    dma = pltpu.SemaphoreType.DMA
    vmem = pl.BlockSpec(memory_space=pltpu.VMEM)
    hbm = pl.BlockSpec(memory_space=pl.ANY)
    found = pl.pallas_call(
        main_kernel,
        out_shape=jax.ShapeDtypeStruct((2 * ROWS, INPUTS), BF),
        in_specs=[hbm, vmem, vmem],
        out_specs=hbm,
        scratch_shapes=[
            pltpu.VMEM((LOCAL, SAMP_DEV), BF),
            pltpu.VMEM((256, 256), BF),
            pltpu.VMEM((16, CHUNK, 4 * NFFT), BF),
            pltpu.VMEM((16, CHANNELS, WIDE), BF),
            pltpu.VMEM((PARTS, 2, 32, LOCAL, WIDE), BF),
            pltpu.VMEM((PARTS, 2, ROWS, WIDE), BF),
            pltpu.VMEM((PARTS, ROWS, WIDE), BF),
            pltpu.VMEM((PARTS, ROWS, WIDE), BF),
            pltpu.VMEM((PARTS, ROWS, WIDE), BF),
            pltpu.VMEM((2, INPUTS, ROWS), BF),
            pltpu.VMEM((INPUTS, WIDE), BF),
            pltpu.VMEM((2 * ROWS, WIDE), BF),
            pltpu.VMEM((8, 2 * ROWS, 256), F32),
            pltpu.VMEM((2, 2 * ROWS, 256), BF),
            dma((PARTS,)),
            dma((PARTS,)),
            dma((PARTS, 4)),
            dma((PARTS,)),
            dma((PARTS, 3)),
            dma((2,)),
        ],
        compiler_params=pltpu.CompilerParams(
            collective_id=0, has_side_effects=True, vmem_limit_bytes=60 << 20
        ),
        name="exchange_correlate",
    )(voltages, coef, assign.reshape(1, INPUTS))

    r = np.arange(256)
    source = ((r % 16) // 2) * 32 + (r % 2) * 16 + r // 16
    perm = jnp.asarray(source[:, None] == r[None, :], BF)
    tile = 128
    placed = pl.pallas_call(
        place_kernel,
        grid=(ROWS // tile,),
        in_specs=[
            pl.BlockSpec((256, 256), lambda i: (0, 0)),
            pl.BlockSpec((2, tile, INPUTS), lambda i: (0, i, 0)),
        ],
        out_specs=pl.BlockSpec((tile, 32, 128), lambda i: (i, 0, 0)),
        out_shape=jax.ShapeDtypeStruct((ROWS, 32, 128), BF),
        compiler_params=pltpu.CompilerParams(vmem_limit_bytes=16 << 20),
        name="place",
    )(perm, found.reshape(2, ROWS, INPUTS))
    return placed.reshape(ROWS, 16, 2, 128).transpose(0, 2, 1, 3).reshape(1, ROWS, 2, INPUTS)


def solution(mesh):
    placed = (P("chan", "tm"), P(), P())
    return jax.shard_map(
        shards, mesh=mesh, in_specs=placed, out_specs=P("chan", "tm", None, None), check_vma=False
    )
```

```python
import jax
import jax.numpy as jnp
import numpy as np
from jax import lax
from jax.experimental import pallas as pl
from jax.experimental.pallas import tpu as pltpu
from jax.sharding import PartitionSpec as P

NFFT = 128
TAPS = 4
SPEC_DEV = 512
SAMP_DEV = 65920
INPUTS = 2048
CHANNELS = 64
TOTAL_SPEC = 1024
ROWS = 1024
LOCAL = 32
PARTS = 4
CHUNK = SPEC_DEV // PARTS
WIDE = 2 * CHUNK
MESH = pl.DeviceIdType.MESH
BF = jnp.bfloat16
F32 = jnp.float32


def filter_window():
    at = np.arange(TAPS * NFFT, dtype=np.float64)
    middle = (TAPS * NFFT - 1) / 2.0
    window = np.sinc((at - middle) / NFFT) * (0.54 - 0.46 * np.cos(np.pi * at / middle))
    return (window / np.sqrt(np.sum(window * window)))[None, :]


def contract_lanes(left, right):
    return lax.dot_general(left, right, (((1,), (1,)), ((), ())), preferred_element_type=F32)


def dot(left, right):
    return jnp.dot(left, right, preferred_element_type=F32)


def main_kernel(
    volt_hbm,
    kept,
    window,
    assign,
    acc,
    right,
    volt,
    perm,
    coef,
    frames,
    chan,
    sendbuf,
    near,
    slab_a,
    slab_b,
    slab_c,
    onehot,
    lower,
    partial,
    volt_sem,
    near_send,
    near_recv,
    slab_send,
    slab_recv,
):
    me = lax.axis_index("chan")
    half = lax.axis_index("tm")
    low = me // 32
    y = (me // 8) % 4
    z = (me // 2) % 4
    core = me % 2
    place = me % 32

    def volt_copy(q):
        first = 0 if q == 0 else (q * CHUNK + 3) * NFFT
        last = ((q + 1) * CHUNK + 3) * NFFT
        part = pl.ds(first, last - first)
        return pltpu.make_async_copy(volt_hbm.at[:, part], volt.at[:, part], volt_sem.at[q])

    for q in range(PARTS):
        volt_copy(q).start()

    def near_device(dy, dz, dc):
        there = (((y + dy) % 4) * 4 + (z + dz) % 4) * 2 + (core + dc) % 2
        return there

    barrier = pltpu.get_barrier_semaphore()

    def greet(k, carry):
        there = near_device(k // 8, (k // 2) % 4, k % 2)
        pl.semaphore_signal(
            barrier, inc=1, device_id=(low * 32 + there, half), device_id_type=MESH
        )
        return carry

    lax.fori_loop(1, 32, greet, 0)
    far = (
        ((1 - low) * 32 + place, half),
        ((1 - low) * 32 + place, 1 - half),
        (low * 32 + place, 1 - half),
    )
    for device in far:
        pl.semaphore_signal(barrier, inc=1, device_id=device, device_id_type=MESH)

    row = lax.broadcasted_iota(jnp.int32, (256, 256), 0)
    col = lax.broadcasted_iota(jnp.int32, (256, 256), 1)
    perm[...] = jnp.where(col == (row & 15) * 16 + (row >> 4), 1.0, 0.0).astype(BF)

    bins = kept[...].astype(F32)
    row = lax.broadcasted_iota(jnp.int32, (2 * CHANNELS, CHANNELS), 0)
    col = lax.broadcasted_iota(jnp.int32, (2 * CHANNELS, CHANNELS), 1)
    own_bin = jnp.sum(jnp.where((row & 63) == col, bins, 0.0), axis=1, keepdims=True)
    row = lax.broadcasted_iota(jnp.int32, (2 * CHANNELS, NFFT), 0)
    col = lax.broadcasted_iota(jnp.int32, (2 * CHANNELS, NFFT), 1)
    turns = col.astype(F32) * own_bin + (row >> 6).astype(F32) * (NFFT / 4.0)
    turns = turns - jnp.floor(turns * (1.0 / NFFT)) * NFFT
    wave = jnp.cos(turns * (2.0 * np.pi / NFFT))
    for tap in range(TAPS):
        lanes = slice(tap * NFFT, (tap + 1) * NFFT)
        coef[:, lanes] = (wave * window[:, lanes]).astype(BF)

    def channelize(q):
        volt_copy(q).wait()
        for ih in range(2):

            def reorder(sb, carry):
                base = (q * CHUNK + sb * 16) * NFFT
                pieces = [
                    volt[ih * 16 : ih * 16 + 16, pl.ds(pl.multiple_of(base + s * NFFT, NFFT), 4 * NFFT)]
                    for s in range(16)
                ]
                moved = dot(perm[...], jnp.concatenate(pieces, axis=0)).astype(BF)
                frames[:, pl.ds(pl.multiple_of(sb * 16, 16), 16), :] = moved.reshape(16, 16, 4 * NFFT)
                return carry

            lax.fori_loop(0, CHUNK // 16, reorder, 0, unroll=True)

            def transform(ip, carry):
                pair = frames[pl.ds(ip * 2, 2)].reshape(2 * CHUNK, 4 * NFFT)
                found = contract_lanes(coef[...], pair).astype(BF)
                for i in range(2):
                    for p in range(2):
                        chan[ip * 2 + i, :, p * CHUNK : (p + 1) * CHUNK] = found[
                            p * CHANNELS : (p + 1) * CHANNELS, i * CHUNK : (i + 1) * CHUNK
                        ]
                return carry

            lax.fori_loop(0, 8, transform, 0, unroll=True)

            for cb in range(4):
                block = chan[:, cb * 16 : cb * 16 + 16, :].reshape(256, WIDE)
                moved = dot(perm[...], block).astype(BF).reshape(16, 16, WIDE)
                sendbuf[q, cb // 2, (cb % 2) * 16 : (cb % 2) * 16 + 16, ih * 16 : ih * 16 + 16, :] = moved

    my_rows = pl.ds(pl.multiple_of(place * LOCAL, LOCAL), LOCAL)

    def self_copy(q):
        return pltpu.make_async_copy(
            sendbuf.at[q, :, place], near.at[q, :, my_rows], near_recv.at[q, y]
        )

    def near_copy(q, dy, dz, dc):
        there = near_device(dy, dz, dc)
        return pltpu.make_async_remote_copy(
            src_ref=sendbuf.at[q, :, there],
            dst_ref=near.at[q, :, my_rows],
            send_sem=near_send.at[q],
            recv_sem=near_recv.at[q, y],
            device_id=(low * 32 + there, half),
            device_id_type=MESH,
        )

    def send_near(q):
        self_copy(q).start()
        if q == 0:

            def first(k, carry):
                near_copy(q, 0, k // 2, k % 2).start()
                return carry

            lax.fori_loop(1, 8, first, 0)

            def second(k, carry):
                near_copy(q, 1 + 2 * (k % 2), (k // 2) % 4, k // 8).start()
                return carry

            lax.fori_loop(0, 16, second, 0)

            def third(k, carry):
                near_copy(q, 2, k // 2, k % 2).start()
                return carry

            lax.fori_loop(0, 8, third, 0)
        else:

            def some(k, carry):
                o = (k * 11) % 32
                near_copy(q, o % 4, (o // 4) % 4, o // 16).start()
                return carry

            lax.fori_loop(1, 32, some, 0)

    def slab_copy(q, group, kind):
        rows = pl.ds(pl.multiple_of(group * 256, 256), 256)
        which = low if kind == 2 else 1 - low
        slab = (slab_a, slab_b, slab_c)[kind]
        return pltpu.make_async_remote_copy(
            src_ref=near.at[q, which, rows],
            dst_ref=slab.at[q, rows],
            send_sem=slab_send.at[q],
            recv_sem=slab_recv.at[q, kind],
            device_id=far[kind],
            device_id_type=MESH,
        )

    def wait_group(q, group):
        rows = pl.ds(pl.multiple_of(group * 256, 256), 256)
        block = near.at[q, :, rows]
        pltpu.make_async_copy(block, block, near_recv.at[q, group]).wait()

    def forward_group(q, step):
        group = (y + (0, 1, 3, 2)[step]) % 4
        wait_group(q, group)
        for kind in range(3):
            slab_copy(q, group, kind).start()

    def forward(q):
        for step in range(4):
            wait_group(q, (y + step) % 4)
        for step in range(4):
            for kind in range(2):
                slab_copy(q, step, kind).start()
        for step in range(4):
            slab_copy(q, step, 2).start()

    def wait_slab(q, kind):
        block = (slab_a, slab_b, slab_c)[kind].at[q]
        pltpu.make_async_copy(block, block, slab_recv.at[q, kind]).wait()

    def reorder_inputs(mine, other):
        def part(t, carry):
            rows = pl.ds(pl.multiple_of(t * 1024, 1024), 1024)
            total = dot(onehot[low, rows, :], mine[...]) + dot(onehot[1 - low, rows, :], other[...])
            right[rows, :] = total.astype(BF)
            return carry

        lax.fori_loop(0, 2, part, 0)

    def reorder_first(other):
        def part(t, carry):
            rows = pl.ds(pl.multiple_of(t * 1024, 1024), 1024)
            partial[rows, :] = dot(onehot[1 - low, rows, :], other[...])
            return carry

        lax.fori_loop(0, 2, part, 0)

    def reorder_second(mine):
        def part(t, carry):
            rows = pl.ds(pl.multiple_of(t * 1024, 1024), 1024)
            total = partial[rows, :] + dot(onehot[low, rows, :], mine[...])
            right[rows, :] = total.astype(BF)
            return carry

        lax.fori_loop(0, 2, part, 0)

    def correlate(first=False):
        for t in range(4):
            block = right[pl.ds(pl.multiple_of(half * ROWS + t * 256, 256), 256), :]
            lower[t * 256 : (t + 1) * 256, :CHUNK] = block[:, CHUNK:]
            lower[t * 256 : (t + 1) * 256, CHUNK:] = -block[:, :CHUNK]

        def tile(n, carry):
            columns = right[pl.ds(pl.multiple_of(n * ROWS, ROWS), ROWS), :]
            for m in range(8):
                if m < 4:
                    rows = right[pl.ds(pl.multiple_of(half * ROWS + m * 256, 256), 256), :]
                else:
                    rows = lower[(m - 4) * 256 : (m - 3) * 256, :]
                found = contract_lanes(rows, columns)
                if first:
                    acc[n, m * 256 : (m + 1) * 256, :] = found
                else:
                    acc[n, m * 256 : (m + 1) * 256, :] += found
            return carry

        lax.fori_loop(0, 2, tile, 0)

    def own_half(q):
        wait_slab(q, 0)
        reorder_inputs(near.at[q, low], slab_a.at[q])

    def other_half(q):
        wait_slab(q, 1)
        wait_slab(q, 2)
        reorder_inputs(slab_c.at[q], slab_b.at[q])

    channelize(0)
    pl.semaphore_wait(barrier, 34)
    send_near(0)
    forward_group(0, 0)
    channelize(1)
    send_near(1)
    for step in range(1, 4):
        forward_group(0, step)
    channelize(2)
    send_near(2)
    channelize(3)
    send_near(3)

    def fill(t, carry):
        rows = pl.ds(pl.multiple_of(t * 256, 256), 256)
        antenna = t * 256 + lax.broadcasted_iota(jnp.int32, (256, ROWS), 0)
        for s in range(2):
            same = antenna == assign[:, s * ROWS : (s + 1) * ROWS]
            onehot[s, rows, :] = jnp.where(same, 1.0, 0.0).astype(BF)
        return carry

    lax.fori_loop(0, 8, fill, 0)
    forward(1)
    own_half(0)
    correlate(True)
    other_half(0)
    correlate()
    forward(2)
    forward(3)

    def middle(q, carry):
        own_half(q)
        correlate()
        other_half(q)
        correlate()
        return carry

    lax.fori_loop(1, 3, middle, 0)
    own_half(3)
    correlate()
    wait_slab(3, 1)
    reorder_first(slab_b.at[3])
    wait_slab(3, 2)
    reorder_second(slab_c.at[3])

    for q in range(PARTS):
        sent = sendbuf.at[q, :, pl.ds(0, 31)]
        pltpu.make_async_copy(sent, sent, near_send.at[q]).wait()
        for slab in (slab_a, slab_b, slab_c):
            pltpu.make_async_copy(slab.at[q], slab.at[q], slab_send.at[q]).wait()


def finish_kernel(perm, acc, right, out_hbm, stage, out_sem):
    half = lax.axis_index("tm")

    def out_copy(t):
        rows = pl.ds(pl.multiple_of(t * 128, 128), 128)
        return pltpu.make_async_copy(stage.at[t % 2], out_hbm.at[rows], out_sem.at[t % 2])

    def tile(t, carry):
        slot = t % 2

        @pl.when(t >= 2)
        def _():
            out_copy(t - 2).wait()

        block = right[pl.ds(pl.multiple_of(half * ROWS + t * 128, 128), 128), :]
        turned = jnp.concatenate([block[:, CHUNK:], -block[:, :CHUNK]], axis=1)
        rows = jnp.concatenate([block, turned], axis=0)
        for jh in range(2):
            found = contract_lanes(rows, right[jh * ROWS : (jh + 1) * ROWS, :])
            pair = []
            for p in range(2):
                before = acc[jh, pl.ds(pl.multiple_of(p * ROWS + t * 128, 128), 128), :]
                total = before + found[p * 128 : (p + 1) * 128]
                pair.append((total * (1.0 / TOTAL_SPEC)).astype(BF))
            for g in range(4):
                sides = [
                    jnp.concatenate(
                        [
                            pair[p][(2 * g + h) * 16 : (2 * g + h + 1) * 16, j * 128 : (j + 1) * 128]
                            for j in range(8)
                            for p in range(2)
                        ],
                        axis=0,
                    )
                    for h in range(2)
                ]
                moved = dot(perm[...], jnp.concatenate(sides, axis=1)).astype(BF)
                for h in range(2):
                    a = (2 * g + h) * 16
                    stage[slot, a : a + 16, jh * 16 : (jh + 1) * 16, :] = moved[
                        :, h * 128 : (h + 1) * 128
                    ].reshape(16, 16, 128)
        out_copy(t).start()
        return carry

    lax.fori_loop(0, 8, tile, 0)
    out_copy(6).wait()
    out_copy(7).wait()


def shards(voltages, kept, assign):
    dma = pltpu.SemaphoreType.DMA
    vmem = pl.BlockSpec(memory_space=pltpu.VMEM)
    hbm = pl.BlockSpec(memory_space=pl.ANY)
    acc, right = pl.pallas_call(
        main_kernel,
        out_shape=[
            pltpu.VMEM((2, 2 * ROWS, INPUTS // 2), F32),
            pltpu.VMEM((INPUTS, WIDE), BF),
        ],
        in_specs=[hbm, vmem, vmem, vmem],
        out_specs=[vmem, vmem],
        scratch_shapes=[
            pltpu.VMEM((LOCAL, SAMP_DEV), BF),
            pltpu.VMEM((256, 256), BF),
            pltpu.VMEM((2 * CHANNELS, TAPS * NFFT), BF),
            pltpu.VMEM((16, CHUNK, 4 * NFFT), BF),
            pltpu.VMEM((16, CHANNELS, WIDE), BF),
            pltpu.VMEM((PARTS, 2, 32, LOCAL, WIDE), BF),
            pltpu.VMEM((PARTS, 2, ROWS, WIDE), BF),
            pltpu.VMEM((PARTS, ROWS, WIDE), BF),
            pltpu.VMEM((PARTS, ROWS, WIDE), BF),
            pltpu.VMEM((PARTS, ROWS, WIDE), BF),
            pltpu.VMEM((2, INPUTS, ROWS), BF),
            pltpu.VMEM((ROWS, WIDE), BF),
            pltpu.VMEM((INPUTS, WIDE), F32),
            dma((PARTS,)),
            dma((PARTS,)),
            dma((PARTS, 4)),
            dma((PARTS,)),
            dma((PARTS, 3)),
        ],
        compiler_params=pltpu.CompilerParams(
            collective_id=0, has_side_effects=True, vmem_limit_bytes=42 << 20
        ),
        name="exchange_correlate",
    )(voltages, kept.reshape(1, CHANNELS), jnp.asarray(filter_window(), F32), assign.reshape(1, INPUTS))

    r = np.arange(256)
    source = ((r % 16) // 2) * 32 + (r % 2) * 16 + r // 16
    perm = jnp.asarray(source[:, None] == r[None, :], BF)
    placed = pl.pallas_call(
        finish_kernel,
        in_specs=[vmem, vmem, vmem],
        out_specs=hbm,
        out_shape=jax.ShapeDtypeStruct((ROWS, 32, 128), BF),
        scratch_shapes=[pltpu.VMEM((2, 128, 32, 128), BF), dma((2,))],
        compiler_params=pltpu.CompilerParams(vmem_limit_bytes=42 << 20),
        name="finish",
    )(
        perm,
        pltpu.with_memory_space_constraint(acc, pltpu.VMEM),
        pltpu.with_memory_space_constraint(right, pltpu.VMEM),
    )
    return placed.reshape(ROWS, 16, 2, 128).transpose(0, 2, 1, 3).reshape(1, ROWS, 2, INPUTS)


def solution(mesh):
    placed = (P("chan", "tm"), P(), P())
    return jax.shard_map(
        shards, mesh=mesh, in_specs=placed, out_specs=P("chan", "tm", None, None), check_vma=False
    )
```

```python
import jax
import jax.numpy as jnp
import numpy as np
from jax import lax
from jax.experimental import pallas as pl
from jax.experimental.pallas import tpu as pltpu
from jax.sharding import PartitionSpec as P

NFFT = 128
TAPS = 4
SPEC_DEV = 512
SAMP_DEV = 65920
INPUTS = 2048
CHANNELS = 64
TOTAL_SPEC = 1024
ROWS = 1024
LOCAL = 32
PARTS = 4
CHUNK = SPEC_DEV // PARTS
WIDE = 2 * CHUNK
MESH = pl.DeviceIdType.MESH
BF = jnp.bfloat16
F32 = jnp.float32


def filter_window():
    at = np.arange(TAPS * NFFT, dtype=np.float64)
    middle = (TAPS * NFFT - 1) / 2.0
    window = np.sinc((at - middle) / NFFT) * (0.54 - 0.46 * np.cos(np.pi * at / middle))
    return (window / np.sqrt(np.sum(window * window)))[None, :]


def contract_lanes(left, right):
    return lax.dot_general(left, right, (((1,), (1,)), ((), ())), preferred_element_type=F32)


def dot(left, right):
    return jnp.dot(left, right, preferred_element_type=F32)


def main_kernel(
    volt_hbm,
    kept,
    window,
    assign,
    acc,
    right,
    volt,
    perm,
    coef,
    frames,
    chan,
    sendbuf,
    near,
    slab_a,
    slab_b,
    slab_c,
    onehot,
    lower,
    partial,
    volt_sem,
    near_send,
    near_recv,
    slab_send,
    slab_recv,
    last_recv,
    crossed,
    cross_recv,
):
    me = lax.axis_index("chan")
    half = lax.axis_index("tm")
    low = me // 32
    y = (me // 8) % 4
    z = (me // 2) % 4
    core = me % 2
    place = me % 32

    def volt_copy(q):
        first = 0 if q == 0 else (q * CHUNK + 3) * NFFT
        last = ((q + 1) * CHUNK + 3) * NFFT
        part = pl.ds(first, last - first)
        return pltpu.make_async_copy(volt_hbm.at[:, part], volt.at[:, part], volt_sem.at[q])

    volt_copy(0).start()

    def near_device(dy, dz, dc):
        there = (((y + dy) % 4) * 4 + (z + dz) % 4) * 2 + (core + dc) % 2
        return there

    barrier = pltpu.get_barrier_semaphore()

    def greet(k, carry):
        there = near_device(k // 8, (k // 2) % 4, k % 2)
        pl.semaphore_signal(
            barrier, inc=1, device_id=(low * 32 + there, half), device_id_type=MESH
        )
        return carry

    lax.fori_loop(1, 32, greet, 0)
    far = (
        ((1 - low) * 32 + place, half),
        ((1 - low) * 32 + place, 1 - half),
        (low * 32 + place, 1 - half),
    )
    for device in far:
        pl.semaphore_signal(barrier, inc=1, device_id=device, device_id_type=MESH)

    row = lax.broadcasted_iota(jnp.int32, (256, 256), 0)
    col = lax.broadcasted_iota(jnp.int32, (256, 256), 1)
    perm[...] = jnp.where(col == (row & 15) * 16 + (row >> 4), 1.0, 0.0).astype(BF)

    bins = kept[...].astype(F32)
    row = lax.broadcasted_iota(jnp.int32, (2 * CHANNELS, CHANNELS), 0)
    col = lax.broadcasted_iota(jnp.int32, (2 * CHANNELS, CHANNELS), 1)
    own_bin = jnp.sum(jnp.where((row & 63) == col, bins, 0.0), axis=1, keepdims=True)
    row = lax.broadcasted_iota(jnp.int32, (2 * CHANNELS, NFFT), 0)
    col = lax.broadcasted_iota(jnp.int32, (2 * CHANNELS, NFFT), 1)
    turns = col.astype(F32) * own_bin + (row >> 6).astype(F32) * (NFFT / 4.0)
    turns = turns - jnp.floor(turns * (1.0 / NFFT)) * NFFT
    wave = jnp.cos(turns * (2.0 * np.pi / NFFT))
    for tap in range(TAPS):
        lanes = slice(tap * NFFT, (tap + 1) * NFFT)
        coef[:, lanes] = (wave * window[:, lanes]).astype(BF)

    def channelize(q):
        volt_copy(q).wait()
        if q == 0:
            for later in range(1, PARTS):
                volt_copy(later).start()
        for ih in range(2):

            def reorder(sb, carry):
                base = (q * CHUNK + sb * 16) * NFFT
                pieces = [
                    volt[ih * 16 : ih * 16 + 16, pl.ds(pl.multiple_of(base + s * NFFT, NFFT), 4 * NFFT)]
                    for s in range(16)
                ]
                moved = dot(perm[...], jnp.concatenate(pieces, axis=0)).astype(BF)
                frames[:, pl.ds(pl.multiple_of(sb * 16, 16), 16), :] = moved.reshape(16, 16, 4 * NFFT)
                return carry

            lax.fori_loop(0, CHUNK // 16, reorder, 0, unroll=True)

            def transform(ip, carry):
                pair = frames[pl.ds(ip * 2, 2)].reshape(2 * CHUNK, 4 * NFFT)
                found = contract_lanes(coef[...], pair).astype(BF)
                for i in range(2):
                    for p in range(2):
                        chan[ip * 2 + i, :, p * CHUNK : (p + 1) * CHUNK] = found[
                            p * CHANNELS : (p + 1) * CHANNELS, i * CHUNK : (i + 1) * CHUNK
                        ]
                return carry

            lax.fori_loop(0, 8, transform, 0, unroll=True)

            for cb in range(4):
                block = chan[:, cb * 16 : cb * 16 + 16, :].reshape(256, WIDE)
                moved = dot(perm[...], block).astype(BF).reshape(16, 16, WIDE)
                sendbuf[q, cb // 2, (cb % 2) * 16 : (cb % 2) * 16 + 16, ih * 16 : ih * 16 + 16, :] = moved

    my_rows = pl.ds(pl.multiple_of(place * LOCAL, LOCAL), LOCAL)

    def self_copy(q):
        return pltpu.make_async_copy(
            sendbuf.at[q, :, place], near.at[q, :, my_rows], near_recv.at[q, y]
        )

    def near_copy(q, dy, dz, dc):
        there = near_device(dy, dz, dc)
        return pltpu.make_async_remote_copy(
            src_ref=sendbuf.at[q, :, there],
            dst_ref=near.at[q, :, my_rows],
            send_sem=near_send.at[q],
            recv_sem=near_recv.at[q, y],
            device_id=(low * 32 + there, half),
            device_id_type=MESH,
        )

    def cross_copy(piece, kind):
        which = low if kind == 2 else 1 - low
        blocks = slice(piece * 8, piece * 8 + 8)
        return pltpu.make_async_remote_copy(
            src_ref=sendbuf.at[0, which, blocks],
            dst_ref=crossed.at[kind, blocks],
            send_sem=slab_send.at[0],
            recv_sem=cross_recv.at[kind],
            device_id=far[kind],
            device_id_type=MESH,
        )

    def spread(kind):
        if kind == 3:
            source, target, sem = sendbuf.at[0, low], near.at[0, low], near_recv.at[0, 0]
        else:
            block = crossed.at[kind]
            pltpu.make_async_copy(block, block, cross_recv.at[kind]).wait()
            source, target = block, (slab_a, slab_b, slab_c)[kind].at[0]
            sem = slab_recv.at[0, kind]
        pltpu.make_async_copy(source.at[place], target.at[my_rows], sem).start()

        def some(k, carry):
            o = (k * 11) % 32
            there = near_device(o % 4, (o // 4) % 4, o // 16)
            pltpu.make_async_remote_copy(
                src_ref=source.at[there],
                dst_ref=target.at[my_rows],
                send_sem=near_send.at[0],
                recv_sem=sem,
                device_id=(low * 32 + there, half),
                device_id_type=MESH,
            ).start()
            return carry

        lax.fori_loop(1, 32, some, 0)

    def some_near(q, first, last):
        if first == 1:
            self_copy(q).start()

        def some(k, carry):
            o = (k * 11) % 32
            near_copy(q, o % 4, (o // 4) % 4, o // 16).start()
            return carry

        lax.fori_loop(first, last, some, 0)

    def slab_copy(q, group, kind):
        rows = pl.ds(pl.multiple_of(group * 256, 256), 256)
        which = low if kind == 2 else 1 - low
        slab = (slab_a, slab_b, slab_c)[kind]
        last = q == PARTS - 1 and kind == 2
        return pltpu.make_async_remote_copy(
            src_ref=near.at[q, which, rows],
            dst_ref=slab.at[q, rows],
            send_sem=slab_send.at[q],
            recv_sem=last_recv.at[group] if last else slab_recv.at[q, kind],
            device_id=far[kind],
            device_id_type=MESH,
        )

    def wait_group(q, group):
        rows = pl.ds(pl.multiple_of(group * 256, 256), 256)
        block = near.at[q, :, rows]
        pltpu.make_async_copy(block, block, near_recv.at[q, group]).wait()

    def forward(q):
        for step in range(4):
            wait_group(q, (y + step) % 4)
        for step in range(4):
            for kind in range(2):
                slab_copy(q, step, kind).start()
        for step in range(4):
            slab_copy(q, step, 2).start()

    def wait_slab(q, kind):
        block = (slab_a, slab_b, slab_c)[kind].at[q]
        pltpu.make_async_copy(block, block, slab_recv.at[q, kind]).wait()

    def reorder_inputs(mine, other):
        def part(t, carry):
            rows = pl.ds(pl.multiple_of(t * 1024, 1024), 1024)
            total = dot(onehot[low, rows, :], mine[...]) + dot(onehot[1 - low, rows, :], other[...])
            right[rows, :] = total.astype(BF)
            return carry

        lax.fori_loop(0, 2, part, 0)

    def reorder_first(other):
        def part(t, carry):
            rows = pl.ds(pl.multiple_of(t * 1024, 1024), 1024)
            partial[rows, :] = dot(onehot[1 - low, rows, :], other[...])
            return carry

        lax.fori_loop(0, 2, part, 0)

    def reorder_second(q):
        for group in range(4):
            inputs = slice(group * 256, (group + 1) * 256)
            block = slab_c.at[q, inputs]
            pltpu.make_async_copy(block, block, last_recv.at[group]).wait()
            for t in range(2):
                rows = slice(t * 1024, (t + 1) * 1024)
                total = partial[rows, :] + dot(onehot[low, rows, inputs], slab_c[q, inputs, :])
                if group == 3:
                    right[rows, :] = total.astype(BF)
                else:
                    partial[rows, :] = total

    def correlate(first=False):
        for t in range(4):
            block = right[pl.ds(pl.multiple_of(half * ROWS + t * 256, 256), 256), :]
            lower[t * 256 : (t + 1) * 256, :CHUNK] = block[:, CHUNK:]
            lower[t * 256 : (t + 1) * 256, CHUNK:] = -block[:, :CHUNK]

        def tile(n, carry):
            columns = right[pl.ds(pl.multiple_of(n * ROWS, ROWS), ROWS), :]
            for m in range(8):
                if m < 4:
                    rows = right[pl.ds(pl.multiple_of(half * ROWS + m * 256, 256), 256), :]
                else:
                    rows = lower[(m - 4) * 256 : (m - 3) * 256, :]
                found = contract_lanes(rows, columns)
                if first:
                    acc[n, m * 256 : (m + 1) * 256, :] = found
                else:
                    acc[n, m * 256 : (m + 1) * 256, :] += found
            return carry

        lax.fori_loop(0, 2, tile, 0)

    def own_half(q):
        wait_slab(q, 0)
        if q == 0:
            block = near.at[0, low]
            pltpu.make_async_copy(block, block, near_recv.at[0, 0]).wait()
        reorder_inputs(near.at[q, low], slab_a.at[q])

    def other_half(q):
        wait_slab(q, 1)
        wait_slab(q, 2)
        reorder_inputs(slab_c.at[q], slab_b.at[q])

    channelize(0)
    pl.semaphore_wait(barrier, 34)
    for piece in range(4):
        for kind in range(3):
            cross_copy(piece, kind).start()
    channelize(1)
    some_near(1, 1, 32)
    spread(3)
    channelize(2)
    some_near(2, 1, 32)
    channelize(3)

    def fill(t, carry):
        rows = pl.ds(pl.multiple_of(t * 256, 256), 256)
        antenna = t * 256 + lax.broadcasted_iota(jnp.int32, (256, ROWS), 0)
        for s in range(2):
            same = antenna == assign[:, s * ROWS : (s + 1) * ROWS]
            onehot[s, rows, :] = jnp.where(same, 1.0, 0.0).astype(BF)
        return carry

    lax.fori_loop(0, 8, fill, 0)
    forward(1)
    for kind in range(3):
        spread(kind)
    some_near(3, 1, 32)
    forward(2)
    own_half(1)
    correlate(True)
    other_half(1)
    correlate()
    forward(3)
    for q in (0, 2):
        own_half(q)
        correlate()
        other_half(q)
        correlate()
    own_half(3)
    correlate()
    wait_slab(3, 1)
    reorder_first(slab_b.at[3])
    reorder_second(3)

    for q in range(PARTS):
        sent = sendbuf.at[q, :, pl.ds(0, 31)]
        for _ in range(2 if q == 0 else 1):
            pltpu.make_async_copy(sent, sent, near_send.at[q]).wait()
        for slab in (slab_a, slab_b, slab_c):
            pltpu.make_async_copy(slab.at[q], slab.at[q], slab_send.at[q]).wait()


def finish_kernel(perm, acc, right, out_hbm, stage, out_sem):
    half = lax.axis_index("tm")

    def out_copy(t):
        return pltpu.make_async_copy(stage.at[t], out_hbm.at[t * 256 : (t + 1) * 256], out_sem.at[t])

    for t in range(4):
        block = right[pl.ds(pl.multiple_of(half * ROWS + t * 256, 256), 256), :]
        turned = jnp.concatenate([block[:, CHUNK:], -block[:, :CHUNK]], axis=1)
        rows = jnp.concatenate([block, turned], axis=0)
        for jh in range(2):
            found = contract_lanes(rows, right[jh * ROWS : (jh + 1) * ROWS, :])
            pair = []
            for p in range(2):
                first = p * ROWS + t * 256
                total = acc[jh, first : first + 256, :] + found[p * 256 : (p + 1) * 256]
                pair.append(total.astype(BF))
            for g in range(8):
                sides = [
                    jnp.concatenate(
                        [
                            pair[p][(2 * g + h) * 16 : (2 * g + h + 1) * 16, j * 128 : (j + 1) * 128]
                            for j in range(8)
                            for p in range(2)
                        ],
                        axis=0,
                    )
                    for h in range(2)
                ]
                moved = dot(perm[...], jnp.concatenate(sides, axis=1)).astype(BF)
                for h in range(2):
                    a = (2 * g + h) * 16
                    stage[t, a : a + 16, jh * 16 : (jh + 1) * 16, :] = moved[
                        :, h * 128 : (h + 1) * 128
                    ].reshape(16, 16, 128)
        out_copy(t).start()
    for t in range(4):
        out_copy(t).wait()


def shards(voltages, kept, assign):
    dma = pltpu.SemaphoreType.DMA
    vmem = pl.BlockSpec(memory_space=pltpu.VMEM)
    hbm = pl.BlockSpec(memory_space=pl.ANY)
    acc, right = pl.pallas_call(
        main_kernel,
        out_shape=[
            pltpu.VMEM((2, 2 * ROWS, INPUTS // 2), F32),
            pltpu.VMEM((INPUTS, WIDE), BF),
        ],
        in_specs=[hbm, vmem, vmem, vmem],
        out_specs=[vmem, vmem],
        scratch_shapes=[
            pltpu.VMEM((LOCAL, SAMP_DEV), BF),
            pltpu.VMEM((256, 256), BF),
            pltpu.VMEM((2 * CHANNELS, TAPS * NFFT), BF),
            pltpu.VMEM((16, CHUNK, 4 * NFFT), BF),
            pltpu.VMEM((16, CHANNELS, WIDE), BF),
            pltpu.VMEM((PARTS, 2, 32, LOCAL, WIDE), BF),
            pltpu.VMEM((PARTS, 2, ROWS, WIDE), BF),
            pltpu.VMEM((PARTS, ROWS, WIDE), BF),
            pltpu.VMEM((PARTS, ROWS, WIDE), BF),
            pltpu.VMEM((PARTS, ROWS, WIDE), BF),
            pltpu.VMEM((2, INPUTS, ROWS), BF),
            pltpu.VMEM((ROWS, WIDE), BF),
            pltpu.VMEM((INPUTS, WIDE), F32),
            dma((PARTS,)),
            dma((PARTS,)),
            dma((PARTS, 4)),
            dma((PARTS,)),
            dma((PARTS, 3)),
            dma((4,)),
            pltpu.VMEM((3, 32, LOCAL, WIDE), BF),
            dma((3,)),
        ],
        compiler_params=pltpu.CompilerParams(
            collective_id=0, has_side_effects=True, vmem_limit_bytes=42 << 20
        ),
        name="exchange_correlate",
    )(voltages, kept.reshape(1, CHANNELS), jnp.asarray(filter_window(), F32), assign.reshape(1, INPUTS))

    r = np.arange(256)
    source = ((r % 16) // 2) * 32 + (r % 2) * 16 + r // 16
    perm = jnp.asarray((source[:, None] == r[None, :]) / TOTAL_SPEC, BF)
    placed = pl.pallas_call(
        finish_kernel,
        in_specs=[vmem, vmem, vmem],
        out_specs=hbm,
        out_shape=jax.ShapeDtypeStruct((ROWS, 32, 128), BF),
        scratch_shapes=[pltpu.VMEM((4, 256, 32, 128), BF), dma((4,))],
        compiler_params=pltpu.CompilerParams(vmem_limit_bytes=42 << 20),
        name="finish",
    )(
        perm,
        pltpu.with_memory_space_constraint(acc, pltpu.VMEM),
        pltpu.with_memory_space_constraint(right, pltpu.VMEM),
    )
    return placed.reshape(ROWS, 16, 2, 128).transpose(0, 2, 1, 3).reshape(1, ROWS, 2, INPUTS)


def solution(mesh):
    placed = (P("chan", "tm"), P(), P())
    return jax.shard_map(
        shards, mesh=mesh, in_specs=placed, out_specs=P("chan", "tm", None, None), check_vma=False
    )
```

```python
import jax
import jax.numpy as jnp
import numpy as np
from jax import lax
from jax.experimental import pallas as pl
from jax.experimental.pallas import tpu as pltpu
from jax.sharding import PartitionSpec as P

NFFT = 128
TAPS = 4
SPEC_DEV = 512
SAMP_DEV = 65920
INPUTS = 2048
CHANNELS = 64
TOTAL_SPEC = 1024
ROWS = 1024
LOCAL = 32
PARTS = 4
CHUNK = SPEC_DEV // PARTS
WIDE = 2 * CHUNK
MESH = pl.DeviceIdType.MESH
BF = jnp.bfloat16
F32 = jnp.float32


def filter_window():
    at = np.arange(TAPS * NFFT, dtype=np.float64)
    middle = (TAPS * NFFT - 1) / 2.0
    window = np.sinc((at - middle) / NFFT) * (0.54 - 0.46 * np.cos(np.pi * at / middle))
    return (window / np.sqrt(np.sum(window * window)))[None, :]


def contract_lanes(left, right):
    return lax.dot_general(left, right, (((1,), (1,)), ((), ())), preferred_element_type=F32)


def dot(left, right):
    return jnp.dot(left, right, preferred_element_type=F32)


def main_kernel(
    volt_hbm,
    kept,
    window,
    assign,
    acc,
    right,
    volt,
    perm,
    coef,
    frames,
    chan,
    sendbuf,
    near,
    slab_a,
    slab_b,
    slab_c,
    onehot,
    lower,
    partial,
    volt_sem,
    near_send,
    near_recv,
    slab_send,
    slab_recv,
    last_recv,
    crossed,
    cross_recv,
):
    me = lax.axis_index("chan")
    half = lax.axis_index("tm")
    low = me // 32
    y = (me // 8) % 4
    z = (me // 2) % 4
    core = me % 2
    place = me % 32

    def volt_copy(q):
        first = 0 if q == 0 else (q * CHUNK + 3) * NFFT
        last = ((q + 1) * CHUNK + 3) * NFFT
        part = pl.ds(first, last - first)
        return pltpu.make_async_copy(volt_hbm.at[:, part], volt.at[:, part], volt_sem.at[q])

    volt_copy(0).start()

    def near_device(dy, dz, dc):
        there = (((y + dy) % 4) * 4 + (z + dz) % 4) * 2 + (core + dc) % 2
        return there

    barrier = pltpu.get_barrier_semaphore()

    def greet(k, carry):
        there = near_device(k // 8, (k // 2) % 4, k % 2)
        pl.semaphore_signal(
            barrier, inc=1, device_id=(low * 32 + there, half), device_id_type=MESH
        )
        return carry

    lax.fori_loop(1, 32, greet, 0)
    far = (
        ((1 - low) * 32 + place, half),
        ((1 - low) * 32 + place, 1 - half),
        (low * 32 + place, 1 - half),
    )
    for device in far:
        pl.semaphore_signal(barrier, inc=1, device_id=device, device_id_type=MESH)

    row = lax.broadcasted_iota(jnp.int32, (256, 256), 0)
    col = lax.broadcasted_iota(jnp.int32, (256, 256), 1)
    perm[...] = jnp.where(col == (row & 15) * 16 + (row >> 4), 1.0, 0.0).astype(BF)

    bins = kept[...].astype(F32)
    row = lax.broadcasted_iota(jnp.int32, (2 * CHANNELS, CHANNELS), 0)
    col = lax.broadcasted_iota(jnp.int32, (2 * CHANNELS, CHANNELS), 1)
    own_bin = jnp.sum(jnp.where((row & 63) == col, bins, 0.0), axis=1, keepdims=True)
    row = lax.broadcasted_iota(jnp.int32, (2 * CHANNELS, NFFT), 0)
    col = lax.broadcasted_iota(jnp.int32, (2 * CHANNELS, NFFT), 1)
    turns = col.astype(F32) * own_bin + (row >> 6).astype(F32) * (NFFT / 4.0)
    turns = turns - jnp.floor(turns * (1.0 / NFFT)) * NFFT
    wave = jnp.cos(turns * (2.0 * np.pi / NFFT))
    for tap in range(TAPS):
        lanes = slice(tap * NFFT, (tap + 1) * NFFT)
        coef[:, lanes] = (wave * window[:, lanes]).astype(BF)

    def channelize(q):
        volt_copy(q).wait()
        if q == 0:
            for later in range(1, PARTS):
                volt_copy(later).start()
        for ih in range(2):

            def reorder(sb, carry):
                base = (q * CHUNK + sb * 16) * NFFT
                pieces = [
                    volt[ih * 16 : ih * 16 + 16, pl.ds(pl.multiple_of(base + s * NFFT, NFFT), 4 * NFFT)]
                    for s in range(16)
                ]
                moved = dot(perm[...], jnp.concatenate(pieces, axis=0)).astype(BF)
                frames[:, pl.ds(pl.multiple_of(sb * 16, 16), 16), :] = moved.reshape(16, 16, 4 * NFFT)
                return carry

            lax.fori_loop(0, CHUNK // 16, reorder, 0, unroll=True)

            def transform(ip, carry):
                pair = frames[pl.ds(ip * 2, 2)].reshape(2 * CHUNK, 4 * NFFT)
                found = contract_lanes(coef[...], pair).astype(BF)
                for i in range(2):
                    for p in range(2):
                        chan[ip * 2 + i, :, p * CHUNK : (p + 1) * CHUNK] = found[
                            p * CHANNELS : (p + 1) * CHANNELS, i * CHUNK : (i + 1) * CHUNK
                        ]
                return carry

            lax.fori_loop(0, 8, transform, 0, unroll=True)

            for cb in range(4):
                block = chan[:, cb * 16 : cb * 16 + 16, :].reshape(256, WIDE)
                moved = dot(perm[...], block).astype(BF).reshape(16, 16, WIDE)
                sendbuf[q, cb // 2, (cb % 2) * 16 : (cb % 2) * 16 + 16, ih * 16 : ih * 16 + 16, :] = moved

    my_rows = pl.ds(pl.multiple_of(place * LOCAL, LOCAL), LOCAL)

    def self_copy(q):
        return pltpu.make_async_copy(
            sendbuf.at[q, :, place], near.at[q, :, my_rows], near_recv.at[q, y]
        )

    def near_copy(q, dy, dz, dc):
        there = near_device(dy, dz, dc)
        return pltpu.make_async_remote_copy(
            src_ref=sendbuf.at[q, :, there],
            dst_ref=near.at[q, :, my_rows],
            send_sem=near_send.at[q],
            recv_sem=near_recv.at[q, y],
            device_id=(low * 32 + there, half),
            device_id_type=MESH,
        )

    def cross_copy(piece, kind):
        which = low if kind == 2 else 1 - low
        blocks = slice(piece * 8, piece * 8 + 8)
        return pltpu.make_async_remote_copy(
            src_ref=sendbuf.at[0, which, blocks],
            dst_ref=crossed.at[kind, blocks],
            send_sem=slab_send.at[0],
            recv_sem=cross_recv.at[kind],
            device_id=far[kind],
            device_id_type=MESH,
        )

    def spread(kind):
        if kind == 3:
            source, target, sem = sendbuf.at[0, low], near.at[0, low], near_recv.at[0, 0]
        else:
            block = crossed.at[kind]
            pltpu.make_async_copy(block, block, cross_recv.at[kind]).wait()
            source, target = block, (slab_a, slab_b, slab_c)[kind].at[0]
            sem = slab_recv.at[0, kind]
        pltpu.make_async_copy(source.at[place], target.at[my_rows], sem).start()

        def some(k, carry):
            o = (k * 11) % 32
            there = near_device(o % 4, (o // 4) % 4, o // 16)
            pltpu.make_async_remote_copy(
                src_ref=source.at[there],
                dst_ref=target.at[my_rows],
                send_sem=near_send.at[0],
                recv_sem=sem,
                device_id=(low * 32 + there, half),
                device_id_type=MESH,
            ).start()
            return carry

        lax.fori_loop(1, 32, some, 0)

    def some_near(q, first, last):
        if first == 1:
            self_copy(q).start()

        def some(k, carry):
            o = (k * 11) % 32
            near_copy(q, o % 4, (o // 4) % 4, o // 16).start()
            return carry

        lax.fori_loop(first, last, some, 0)

    def slab_copy(q, group, kind):
        rows = pl.ds(pl.multiple_of(group * 256, 256), 256)
        which = low if kind == 2 else 1 - low
        slab = (slab_a, slab_b, slab_c)[kind]
        last = q == PARTS - 1 and kind == 2
        return pltpu.make_async_remote_copy(
            src_ref=near.at[q, which, rows],
            dst_ref=slab.at[q, rows],
            send_sem=slab_send.at[q],
            recv_sem=last_recv.at[group] if last else slab_recv.at[q, kind],
            device_id=far[kind],
            device_id_type=MESH,
        )

    def wait_group(q, group):
        rows = pl.ds(pl.multiple_of(group * 256, 256), 256)
        block = near.at[q, :, rows]
        pltpu.make_async_copy(block, block, near_recv.at[q, group]).wait()

    def forward(q):
        for step in range(4):
            wait_group(q, (y + step) % 4)
        for step in range(4):
            for kind in range(2):
                slab_copy(q, step, kind).start()
        for step in range(4):
            slab_copy(q, step, 2).start()

    def wait_slab(q, kind):
        block = (slab_a, slab_b, slab_c)[kind].at[q]
        pltpu.make_async_copy(block, block, slab_recv.at[q, kind]).wait()

    def reorder_inputs(mine, other):
        def part(t, carry):
            rows = pl.ds(pl.multiple_of(t * 1024, 1024), 1024)
            total = dot(onehot[low, rows, :], mine[...]) + dot(onehot[1 - low, rows, :], other[...])
            right[rows, :] = total.astype(BF)
            return carry

        lax.fori_loop(0, 2, part, 0)

    def reorder_first(other):
        def part(t, carry):
            rows = pl.ds(pl.multiple_of(t * 1024, 1024), 1024)
            partial[rows, :] = dot(onehot[1 - low, rows, :], other[...])
            return carry

        lax.fori_loop(0, 2, part, 0)

    def reorder_second(q):
        for group in range(4):
            inputs = slice(group * 256, (group + 1) * 256)
            block = slab_c.at[q, inputs]
            pltpu.make_async_copy(block, block, last_recv.at[group]).wait()
            for t in range(2):
                rows = slice(t * 1024, (t + 1) * 1024)
                total = partial[rows, :] + dot(onehot[low, rows, inputs], slab_c[q, inputs, :])
                if group == 3:
                    right[rows, :] = total.astype(BF)
                else:
                    partial[rows, :] = total

    def correlate(first=False):
        for t in range(4):
            block = right[pl.ds(pl.multiple_of(half * ROWS + t * 256, 256), 256), :]
            lower[t * 256 : (t + 1) * 256, :CHUNK] = block[:, CHUNK:]
            lower[t * 256 : (t + 1) * 256, CHUNK:] = -block[:, :CHUNK]

        def tile(n, carry):
            columns = right[pl.ds(pl.multiple_of(n * ROWS, ROWS), ROWS), :]
            for m in range(8):
                if m < 4:
                    rows = right[pl.ds(pl.multiple_of(half * ROWS + m * 256, 256), 256), :]
                else:
                    rows = lower[(m - 4) * 256 : (m - 3) * 256, :]
                found = contract_lanes(rows, columns)
                if first:
                    acc[n, m * 256 : (m + 1) * 256, :] = found
                else:
                    acc[n, m * 256 : (m + 1) * 256, :] += found
            return carry

        lax.fori_loop(0, 2, tile, 0)

    def own_half(q):
        wait_slab(q, 0)
        if q == 0:
            block = near.at[0, low]
            pltpu.make_async_copy(block, block, near_recv.at[0, 0]).wait()
        reorder_inputs(near.at[q, low], slab_a.at[q])

    def other_half(q):
        wait_slab(q, 1)
        wait_slab(q, 2)
        reorder_inputs(slab_c.at[q], slab_b.at[q])

    channelize(0)
    pl.semaphore_wait(barrier, 34)
    for piece in range(4):
        for kind in range(3):
            cross_copy(piece, kind).start()
    channelize(1)
    some_near(1, 1, 32)
    spread(3)
    channelize(2)
    some_near(2, 1, 32)
    channelize(3)

    def fill(t, carry):
        rows = pl.ds(pl.multiple_of(t * 256, 256), 256)
        antenna = t * 256 + lax.broadcasted_iota(jnp.int32, (256, ROWS), 0)
        for s in range(2):
            same = antenna == assign[:, s * ROWS : (s + 1) * ROWS]
            onehot[s, rows, :] = jnp.where(same, 1.0, 0.0).astype(BF)
        return carry

    lax.fori_loop(0, 8, fill, 0)
    forward(1)
    for kind in range(3):
        spread(kind)
    some_near(3, 1, 32)
    forward(2)
    own_half(1)
    correlate(True)
    other_half(1)
    correlate()
    forward(3)
    for q in (0, 2):
        own_half(q)
        correlate()
        other_half(q)
        correlate()
    own_half(3)
    correlate()
    wait_slab(3, 1)
    reorder_first(slab_b.at[3])
    reorder_second(3)

    for q in range(PARTS):
        sent = sendbuf.at[q, :, pl.ds(0, 31)]
        for _ in range(2 if q == 0 else 1):
            pltpu.make_async_copy(sent, sent, near_send.at[q]).wait()
        for slab in (slab_a, slab_b, slab_c):
            pltpu.make_async_copy(slab.at[q], slab.at[q], slab_send.at[q]).wait()


TILE = 128
STEP = 36


def finish_kernel(acc, right, out_hbm, wide, stage, out_sem):
    half = lax.axis_index("tm")

    def out_copy(t):
        return pltpu.make_async_copy(
            stage.at[t], out_hbm.at[t * TILE : (t + 1) * TILE], out_sem.at[t]
        )

    for t in range(ROWS // TILE):
        block = right[pl.ds(pl.multiple_of(half * ROWS + t * TILE, TILE), TILE), :]
        turned = jnp.concatenate([block[:, CHUNK:], -block[:, :CHUNK]], axis=1)
        rows = jnp.concatenate([block, turned], axis=0)
        for jh in range(2):
            found = contract_lanes(rows, right[jh * ROWS : (jh + 1) * ROWS, :])
            for p in range(2):
                first = p * ROWS + t * TILE
                total = acc[jh, first : first + TILE, :] + found[p * TILE : (p + 1) * TILE]
                for j in range(8):
                    place = pl.ds(2 * (jh * 8 + j) + p, TILE, stride=STEP)
                    wide[t % 2, place, :] = total[:, j * 128 : (j + 1) * 128]
        for a in range(TILE):
            stage[t, a] = (wide[t % 2, a * STEP : a * STEP + 32, :] * (1.0 / TOTAL_SPEC)).astype(BF)
        out_copy(t).start()
    for t in range(ROWS // TILE):
        out_copy(t).wait()


def shards(voltages, kept, assign):
    dma = pltpu.SemaphoreType.DMA
    vmem = pl.BlockSpec(memory_space=pltpu.VMEM)
    hbm = pl.BlockSpec(memory_space=pl.ANY)
    acc, right = pl.pallas_call(
        main_kernel,
        out_shape=[
            pltpu.VMEM((2, 2 * ROWS, INPUTS // 2), F32),
            pltpu.VMEM((INPUTS, WIDE), BF),
        ],
        in_specs=[hbm, vmem, vmem, vmem],
        out_specs=[vmem, vmem],
        scratch_shapes=[
            pltpu.VMEM((LOCAL, SAMP_DEV), BF),
            pltpu.VMEM((256, 256), BF),
            pltpu.VMEM((2 * CHANNELS, TAPS * NFFT), BF),
            pltpu.VMEM((16, CHUNK, 4 * NFFT), BF),
            pltpu.VMEM((16, CHANNELS, WIDE), BF),
            pltpu.VMEM((PARTS, 2, 32, LOCAL, WIDE), BF),
            pltpu.VMEM((PARTS, 2, ROWS, WIDE), BF),
            pltpu.VMEM((PARTS, ROWS, WIDE), BF),
            pltpu.VMEM((PARTS, ROWS, WIDE), BF),
            pltpu.VMEM((PARTS, ROWS, WIDE), BF),
            pltpu.VMEM((2, INPUTS, ROWS), BF),
            pltpu.VMEM((ROWS, WIDE), BF),
            pltpu.VMEM((INPUTS, WIDE), F32),
            dma((PARTS,)),
            dma((PARTS,)),
            dma((PARTS, 4)),
            dma((PARTS,)),
            dma((PARTS, 3)),
            dma((4,)),
            pltpu.VMEM((3, 32, LOCAL, WIDE), BF),
            dma((3,)),
        ],
        compiler_params=pltpu.CompilerParams(
            collective_id=0, has_side_effects=True, vmem_limit_bytes=42 << 20
        ),
        name="exchange_correlate",
    )(voltages, kept.reshape(1, CHANNELS), jnp.asarray(filter_window(), F32), assign.reshape(1, INPUTS))

    placed = pl.pallas_call(
        finish_kernel,
        in_specs=[vmem, vmem],
        out_specs=hbm,
        out_shape=jax.ShapeDtypeStruct((ROWS, 32, 128), BF),
        scratch_shapes=[
            pltpu.VMEM((2, TILE * STEP, 128), F32),
            pltpu.VMEM((ROWS // TILE, TILE, 32, 128), BF),
            dma((ROWS // TILE,)),
        ],
        compiler_params=pltpu.CompilerParams(vmem_limit_bytes=42 << 20),
        name="finish",
    )(
        pltpu.with_memory_space_constraint(acc, pltpu.VMEM),
        pltpu.with_memory_space_constraint(right, pltpu.VMEM),
    )
    return placed.reshape(ROWS, 16, 2, 128).transpose(0, 2, 1, 3).reshape(1, ROWS, 2, INPUTS)


def solution(mesh):
    placed = (P("chan", "tm"), P(), P())
    return jax.shard_map(
        shards, mesh=mesh, in_specs=placed, out_specs=P("chan", "tm", None, None), check_vma=False
    )
```

```python
import jax
import jax.numpy as jnp
import numpy as np
from jax import lax
from jax.experimental import pallas as pl
from jax.experimental.pallas import tpu as pltpu
from jax.sharding import PartitionSpec as P

NFFT = 128
TAPS = 4
SPEC_DEV = 512
SAMP_DEV = 65920
INPUTS = 2048
CHANNELS = 64
TOTAL_SPEC = 1024
ROWS = 1024
LOCAL = 32
PARTS = 4
CHUNK = SPEC_DEV // PARTS
WIDE = 2 * CHUNK
MESH = pl.DeviceIdType.MESH
BF = jnp.bfloat16
F32 = jnp.float32


def filter_window():
    at = np.arange(TAPS * NFFT, dtype=np.float64)
    middle = (TAPS * NFFT - 1) / 2.0
    window = np.sinc((at - middle) / NFFT) * (0.54 - 0.46 * np.cos(np.pi * at / middle))
    return (window / np.sqrt(np.sum(window * window)))[None, :]


def contract_lanes(left, right):
    return lax.dot_general(left, right, (((1,), (1,)), ((), ())), preferred_element_type=F32)


def dot(left, right):
    return jnp.dot(left, right, preferred_element_type=F32)


def main_kernel(
    volt_hbm,
    kept,
    window,
    assign,
    acc,
    right,
    volt,
    perm,
    coef,
    frames,
    chan,
    sendbuf,
    near,
    slab_a,
    slab_b,
    slab_c,
    onehot,
    lower,
    partial,
    volt_sem,
    near_send,
    near_recv,
    slab_send,
    slab_recv,
    last_recv,
    crossed,
    cross_recv,
):
    me = lax.axis_index("chan")
    half = lax.axis_index("tm")
    low = me // 32
    y = (me // 8) % 4
    z = (me // 2) % 4
    core = me % 2
    place = me % 32

    def volt_copy(q):
        first = 0 if q == 0 else (q * CHUNK + 3) * NFFT
        last = ((q + 1) * CHUNK + 3) * NFFT
        part = pl.ds(first, last - first)
        return pltpu.make_async_copy(volt_hbm.at[:, part], volt.at[:, part], volt_sem.at[q])

    volt_copy(0).start()

    def near_device(dy, dz, dc):
        there = (((y + dy) % 4) * 4 + (z + dz) % 4) * 2 + (core + dc) % 2
        return there

    barrier = pltpu.get_barrier_semaphore()

    def greet(k, carry):
        there = near_device(k // 8, (k // 2) % 4, k % 2)
        pl.semaphore_signal(
            barrier, inc=1, device_id=(low * 32 + there, half), device_id_type=MESH
        )
        return carry

    lax.fori_loop(1, 32, greet, 0)
    far = (
        ((1 - low) * 32 + place, half),
        ((1 - low) * 32 + place, 1 - half),
        (low * 32 + place, 1 - half),
    )
    for device in far:
        pl.semaphore_signal(barrier, inc=1, device_id=device, device_id_type=MESH)

    row = lax.broadcasted_iota(jnp.int32, (256, 256), 0)
    col = lax.broadcasted_iota(jnp.int32, (256, 256), 1)
    perm[...] = jnp.where(col == (row & 15) * 16 + (row >> 4), 1.0, 0.0).astype(BF)

    bins = kept[...].astype(F32)
    row = lax.broadcasted_iota(jnp.int32, (2 * CHANNELS, CHANNELS), 0)
    col = lax.broadcasted_iota(jnp.int32, (2 * CHANNELS, CHANNELS), 1)
    own_bin = jnp.sum(jnp.where((row & 63) == col, bins, 0.0), axis=1, keepdims=True)
    row = lax.broadcasted_iota(jnp.int32, (2 * CHANNELS, NFFT), 0)
    col = lax.broadcasted_iota(jnp.int32, (2 * CHANNELS, NFFT), 1)
    turns = col.astype(F32) * own_bin + (row >> 6).astype(F32) * (NFFT / 4.0)
    turns = turns - jnp.floor(turns * (1.0 / NFFT)) * NFFT
    wave = jnp.cos(turns * (2.0 * np.pi / NFFT))
    for tap in range(TAPS):
        lanes = slice(tap * NFFT, (tap + 1) * NFFT)
        coef[:, lanes] = (wave * window[:, lanes]).astype(BF)

    def channelize(q):
        volt_copy(q).wait()
        if q == 0:
            for later in range(1, PARTS):
                volt_copy(later).start()
        for ih in range(2):

            def reorder(sb, carry):
                base = (q * CHUNK + sb * 16) * NFFT
                pieces = [
                    volt[ih * 16 : ih * 16 + 16, pl.ds(pl.multiple_of(base + s * NFFT, NFFT), 4 * NFFT)]
                    for s in range(16)
                ]
                moved = dot(perm[...], jnp.concatenate(pieces, axis=0)).astype(BF)
                frames[:, pl.ds(pl.multiple_of(sb * 16, 16), 16), :] = moved.reshape(16, 16, 4 * NFFT)
                return carry

            lax.fori_loop(0, CHUNK // 16, reorder, 0, unroll=True)

            def transform(ip, carry):
                pair = frames[pl.ds(ip * 2, 2)].reshape(2 * CHUNK, 4 * NFFT)
                found = contract_lanes(coef[...], pair).astype(BF)
                for i in range(2):
                    for p in range(2):
                        chan[ip * 2 + i, :, p * CHUNK : (p + 1) * CHUNK] = found[
                            p * CHANNELS : (p + 1) * CHANNELS, i * CHUNK : (i + 1) * CHUNK
                        ]
                return carry

            lax.fori_loop(0, 8, transform, 0, unroll=True)

            for cb in range(4):
                block = chan[:, cb * 16 : cb * 16 + 16, :].reshape(256, WIDE)
                moved = dot(perm[...], block).astype(BF).reshape(16, 16, WIDE)
                sendbuf[q, cb // 2, (cb % 2) * 16 : (cb % 2) * 16 + 16, ih * 16 : ih * 16 + 16, :] = moved

    my_rows = pl.ds(pl.multiple_of(place * LOCAL, LOCAL), LOCAL)

    def self_copy(q):
        return pltpu.make_async_copy(
            sendbuf.at[q, :, place], near.at[q, :, my_rows], near_recv.at[q, y]
        )

    def near_copy(q, dy, dz, dc):
        there = near_device(dy, dz, dc)
        return pltpu.make_async_remote_copy(
            src_ref=sendbuf.at[q, :, there],
            dst_ref=near.at[q, :, my_rows],
            send_sem=near_send.at[q],
            recv_sem=near_recv.at[q, y],
            device_id=(low * 32 + there, half),
            device_id_type=MESH,
        )

    def cross_copy(piece, kind):
        which = low if kind == 2 else 1 - low
        blocks = slice(piece * 8, piece * 8 + 8)
        return pltpu.make_async_remote_copy(
            src_ref=sendbuf.at[0, which, blocks],
            dst_ref=crossed.at[kind, blocks],
            send_sem=slab_send.at[0],
            recv_sem=cross_recv.at[kind],
            device_id=far[kind],
            device_id_type=MESH,
        )

    def spread(kind):
        if kind == 3:
            source, target, sem = sendbuf.at[0, low], near.at[0, low], near_recv.at[0, 0]
        else:
            block = crossed.at[kind]
            pltpu.make_async_copy(block, block, cross_recv.at[kind]).wait()
            source, target = block, (slab_a, slab_b, slab_c)[kind].at[0]
            sem = slab_recv.at[0, kind]
        pltpu.make_async_copy(source.at[place], target.at[my_rows], sem).start()

        def some(k, carry):
            o = (k * 11) % 32
            there = near_device(o % 4, (o // 4) % 4, o // 16)
            pltpu.make_async_remote_copy(
                src_ref=source.at[there],
                dst_ref=target.at[my_rows],
                send_sem=near_send.at[0],
                recv_sem=sem,
                device_id=(low * 32 + there, half),
                device_id_type=MESH,
            ).start()
            return carry

        lax.fori_loop(1, 32, some, 0)

    def some_near(q, first, last):
        if first == 1:
            self_copy(q).start()

        def some(k, carry):
            o = (k * 11) % 32
            near_copy(q, o % 4, (o // 4) % 4, o // 16).start()
            return carry

        lax.fori_loop(first, last, some, 0)

    def slab_copy(q, piece, kind):
        rows = pl.ds(piece * 128, 128)
        group = piece // 2
        which = low if kind == 2 else 1 - low
        slab = (slab_a, slab_b, slab_c)[kind]
        last = q == PARTS - 1 and kind == 2
        return pltpu.make_async_remote_copy(
            src_ref=near.at[q, which, rows],
            dst_ref=slab.at[q, rows],
            send_sem=slab_send.at[q],
            recv_sem=last_recv.at[group] if last else slab_recv.at[q, kind],
            device_id=far[kind],
            device_id_type=MESH,
        )

    def wait_group(q, group):
        rows = pl.ds(pl.multiple_of(group * 256, 256), 256)
        block = near.at[q, :, rows]
        pltpu.make_async_copy(block, block, near_recv.at[q, group]).wait()

    def forward(q):
        for step in range(4):
            wait_group(q, (y + step) % 4)
        for piece in range(8):
            for kind in range(2):
                slab_copy(q, piece, kind).start()
        for piece in range(8):
            slab_copy(q, piece, 2).start()

    def wait_slab(q, kind):
        block = (slab_a, slab_b, slab_c)[kind].at[q]
        pltpu.make_async_copy(block, block, slab_recv.at[q, kind]).wait()

    def reorder_inputs(mine, other):
        def part(t, carry):
            rows = pl.ds(pl.multiple_of(t * 1024, 1024), 1024)
            total = dot(onehot[low, rows, :], mine[...]) + dot(onehot[1 - low, rows, :], other[...])
            right[rows, :] = total.astype(BF)
            return carry

        lax.fori_loop(0, 2, part, 0)

    def reorder_first(other):
        def part(t, carry):
            rows = pl.ds(pl.multiple_of(t * 1024, 1024), 1024)
            partial[rows, :] = dot(onehot[1 - low, rows, :], other[...])
            return carry

        lax.fori_loop(0, 2, part, 0)

    def reorder_second(q):
        for group in range(4):
            inputs = slice(group * 256, (group + 1) * 256)
            block = slab_c.at[q, inputs]
            pltpu.make_async_copy(block, block, last_recv.at[group]).wait()
            for t in range(2):
                rows = slice(t * 1024, (t + 1) * 1024)
                total = partial[rows, :] + dot(onehot[low, rows, inputs], slab_c[q, inputs, :])
                if group == 3:
                    right[rows, :] = total.astype(BF)
                else:
                    partial[rows, :] = total

    def correlate(first=False):
        for t in range(4):
            block = right[pl.ds(pl.multiple_of(half * ROWS + t * 256, 256), 256), :]
            lower[t * 256 : (t + 1) * 256, :CHUNK] = block[:, CHUNK:]
            lower[t * 256 : (t + 1) * 256, CHUNK:] = -block[:, :CHUNK]

        def tile(n, carry):
            columns = right[pl.ds(pl.multiple_of(n * ROWS, ROWS), ROWS), :]
            for m in range(8):
                if m < 4:
                    rows = right[pl.ds(pl.multiple_of(half * ROWS + m * 256, 256), 256), :]
                else:
                    rows = lower[(m - 4) * 256 : (m - 3) * 256, :]
                found = contract_lanes(rows, columns)
                if first:
                    acc[n, m * 256 : (m + 1) * 256, :] = found
                else:
                    acc[n, m * 256 : (m + 1) * 256, :] += found
            return carry

        lax.fori_loop(0, 2, tile, 0)

    def own_half(q):
        wait_slab(q, 0)
        if q == 0:
            block = near.at[0, low]
            pltpu.make_async_copy(block, block, near_recv.at[0, 0]).wait()
        reorder_inputs(near.at[q, low], slab_a.at[q])

    def other_half(q):
        wait_slab(q, 1)
        wait_slab(q, 2)
        reorder_inputs(slab_c.at[q], slab_b.at[q])

    channelize(0)
    pl.semaphore_wait(barrier, 34)
    for piece in range(4):
        for kind in range(3):
            cross_copy(piece, kind).start()
    channelize(1)
    some_near(1, 1, 32)
    spread(3)
    channelize(2)
    some_near(2, 1, 32)
    channelize(3)

    def fill(t, carry):
        rows = pl.ds(pl.multiple_of(t * 256, 256), 256)
        antenna = t * 256 + lax.broadcasted_iota(jnp.int32, (256, ROWS), 0)
        for s in range(2):
            same = antenna == assign[:, s * ROWS : (s + 1) * ROWS]
            onehot[s, rows, :] = jnp.where(same, 1.0, 0.0).astype(BF)
        return carry

    lax.fori_loop(0, 8, fill, 0)
    forward(1)
    for kind in range(3):
        spread(kind)
    some_near(3, 1, 32)
    forward(2)
    own_half(1)
    correlate(True)
    other_half(1)
    correlate()
    forward(3)
    for q in (0, 2):
        own_half(q)
        correlate()
        other_half(q)
        correlate()
    own_half(3)
    correlate()
    wait_slab(3, 1)
    reorder_first(slab_b.at[3])
    reorder_second(3)

    for q in range(PARTS):
        sent = sendbuf.at[q, :, pl.ds(0, 31)]
        for _ in range(2 if q == 0 else 1):
            pltpu.make_async_copy(sent, sent, near_send.at[q]).wait()
        for slab in (slab_a, slab_b, slab_c):
            pltpu.make_async_copy(slab.at[q], slab.at[q], slab_send.at[q]).wait()


TILE = 128
STEP = 36


def finish_kernel(acc, right, out_hbm, wide, stage, out_sem):
    half = lax.axis_index("tm")

    def out_copy(t):
        return pltpu.make_async_copy(
            stage.at[t], out_hbm.at[t * TILE : (t + 1) * TILE], out_sem.at[t]
        )

    for t in range(ROWS // TILE):
        block = right[pl.ds(pl.multiple_of(half * ROWS + t * TILE, TILE), TILE), :]
        turned = jnp.concatenate([block[:, CHUNK:], -block[:, :CHUNK]], axis=1)
        rows = jnp.concatenate([block, turned], axis=0)
        for jh in range(2):
            found = contract_lanes(rows, right[jh * ROWS : (jh + 1) * ROWS, :])
            for p in range(2):
                first = p * ROWS + t * TILE
                total = acc[jh, first : first + TILE, :] + found[p * TILE : (p + 1) * TILE]
                for j in range(8):
                    place = pl.ds(2 * (jh * 8 + j) + p, TILE, stride=STEP)
                    wide[t % 2, place, :] = total[:, j * 128 : (j + 1) * 128]
        for a in range(TILE):
            stage[t, a] = (wide[t % 2, a * STEP : a * STEP + 32, :] * (1.0 / TOTAL_SPEC)).astype(BF)
        out_copy(t).start()
    for t in range(ROWS // TILE):
        out_copy(t).wait()


def shards(voltages, kept, assign):
    dma = pltpu.SemaphoreType.DMA
    vmem = pl.BlockSpec(memory_space=pltpu.VMEM)
    hbm = pl.BlockSpec(memory_space=pl.ANY)
    acc, right = pl.pallas_call(
        main_kernel,
        out_shape=[
            pltpu.VMEM((2, 2 * ROWS, INPUTS // 2), F32),
            pltpu.VMEM((INPUTS, WIDE), BF),
        ],
        in_specs=[hbm, vmem, vmem, vmem],
        out_specs=[vmem, vmem],
        scratch_shapes=[
            pltpu.VMEM((LOCAL, SAMP_DEV), BF),
            pltpu.VMEM((256, 256), BF),
            pltpu.VMEM((2 * CHANNELS, TAPS * NFFT), BF),
            pltpu.VMEM((16, CHUNK, 4 * NFFT), BF),
            pltpu.VMEM((16, CHANNELS, WIDE), BF),
            pltpu.VMEM((PARTS, 2, 32, LOCAL, WIDE), BF),
            pltpu.VMEM((PARTS, 2, ROWS, WIDE), BF),
            pltpu.VMEM((PARTS, ROWS, WIDE), BF),
            pltpu.VMEM((PARTS, ROWS, WIDE), BF),
            pltpu.VMEM((PARTS, ROWS, WIDE), BF),
            pltpu.VMEM((2, INPUTS, ROWS), BF),
            pltpu.VMEM((ROWS, WIDE), BF),
            pltpu.VMEM((INPUTS, WIDE), F32),
            dma((PARTS,)),
            dma((PARTS,)),
            dma((PARTS, 4)),
            dma((PARTS,)),
            dma((PARTS, 3)),
            dma((4,)),
            pltpu.VMEM((3, 32, LOCAL, WIDE), BF),
            dma((3,)),
        ],
        compiler_params=pltpu.CompilerParams(
            collective_id=0, has_side_effects=True, vmem_limit_bytes=42 << 20
        ),
        name="exchange_correlate",
    )(voltages, kept.reshape(1, CHANNELS), jnp.asarray(filter_window(), F32), assign.reshape(1, INPUTS))

    placed = pl.pallas_call(
        finish_kernel,
        in_specs=[vmem, vmem],
        out_specs=hbm,
        out_shape=jax.ShapeDtypeStruct((ROWS, 32, 128), BF),
        scratch_shapes=[
            pltpu.VMEM((2, TILE * STEP, 128), F32),
            pltpu.VMEM((ROWS // TILE, TILE, 32, 128), BF),
            dma((ROWS // TILE,)),
        ],
        compiler_params=pltpu.CompilerParams(vmem_limit_bytes=42 << 20),
        name="finish",
    )(
        pltpu.with_memory_space_constraint(acc, pltpu.VMEM),
        pltpu.with_memory_space_constraint(right, pltpu.VMEM),
    )
    return placed.reshape(ROWS, 16, 2, 128).transpose(0, 2, 1, 3).reshape(1, ROWS, 2, INPUTS)


def solution(mesh):
    placed = (P("chan", "tm"), P(), P())
    return jax.shard_map(
        shards, mesh=mesh, in_specs=placed, out_specs=P("chan", "tm", None, None), check_vma=False
    )
```
